32 devices in a mesh: groups: 2 (over y), cells: 4 (over z), tm: 2 (over x), cls: 2 (over core).
Axes of the slice: x: 2, y: 2, z: 4, core: 2. Of those that a mesh axis runs over, the one named last changes fastest.
Arguments:
- start_density: float32 [128, 4096], P(('groups', 'cls'), 'cells'), parts along dimension 0, may hold values from 0.1 to 2
- final_value: float32 [128, 4096], P(('groups', 'cls'), 'cells'), parts along dimension 0, may hold values from 0 to 212
- congestion: float32 [4, 4096], P(('groups', 'tm'), 'cells'), parts along dimension 0, may hold values from 0.1 to 10
- capacity: float32 [8192], P(('groups', 'cells')), parts along dimension 0, may hold values from 0.5 to 4
- trans_values: bfloat16 [64, 128, 128], P(('groups', 'cells')), parts along dimension 0, may hold values from 0.00015544891 to 0.0046691895
- src_local: int32 [64], P(('groups', 'cells')), parts along dimension 0, may hold values from 0 to 7
- dst_local: int32 [64], P(('groups', 'cells')), parts along dimension 0, may hold values from 0 to 7
- bucket_len: int32 [32], P(('groups', 'cells')), parts along dimension 0, may hold values from 0 to 2, as said below
Outputs:
- density: float32 [4, 64, 4096], P(('groups', 'tm'), 'cls', 'cells'), parts along dimension 0
- class_mean: float32 [4, 4096], P(('groups', 'tm'), 'cells'), parts along dimension 0
- values: float32 [4, 64, 4096], P(('groups', 'tm'), 'cls', 'cells'), parts along dimension 0
The draws below stay inside these ranges and needn't reach their ends.
There are 2 independent parts, one for each index of `groups`. The reference program is written for one: setup_inputs(seed, part) draws one part's arguments, and reference() takes and returns one part's arrays. A program takes and returns all parts, laid end to end along the dimension named above; each array names one. Nothing has to cross between parts.
Inputs may be any that keep to these rules, and one draw needn't show every extreme that they name: bucket_len[d * 4 + d] = 2 for every owner d: each owner has 2 live slots into its own blocks.
All inputs are finite; a program needn't handle non-finite values.
Results may differ from the reference program's by a relative error of at most 0.00071.
Values may be sent and summed in bfloat16 or wider, within the bound.
A program may use at most 64 MiB of HBM per device.

```python
import math
import jax
import jax.numpy as jnp
from jax import lax

BS = 128
BLK_DEV = 8
CAP = 2
CLASSES = 64
STEPS = 2
CELLS = 4096
EDGE_DEV = 8
EDGES = 32
N_CELLS = 4


def draw_bucket_len(key, part):
    lengths = jax.random.randint(key, (N_CELLS, N_CELLS), 0, CAP + 1, dtype=jnp.int32)
    diagonal = jnp.eye(N_CELLS, dtype=jnp.int32) > 0
    filled = jnp.where(diagonal, jnp.full_like(lengths, CAP), lengths)
    return filled.reshape(N_CELLS * N_CELLS).astype(jnp.int32)


def draw_final_value(key, part):
    cell_key = jax.random.fold_in(key, 11)
    spread = jax.random.uniform(cell_key, (CLASSES, CELLS), jnp.float32, 0.0, 2.0)
    return spread.astype(jnp.float32)


def touch_ends(array, stream_key, low, top_value):
    extent = array.shape
    place = [jax.random.randint(jax.random.fold_in(stream_key, axis), (), 0, extent[axis]) for axis in range(len(extent))]
    array = array.at[tuple(place)].set(low)
    longest = extent.index(max(extent))
    place[longest] = (place[longest] + 1) % extent[longest]
    return array.at[tuple(place)].set(top_value)


def shard_levels(key, shape, cuts, smallest, largest):
    def one(position, shards_of):
        heights = jax.random.uniform(jax.random.fold_in(jax.random.fold_in(key, 6), position), (shards_of,), jnp.float32, smallest / len(cuts), largest / len(cuts))
        return jnp.repeat(jnp.exp(heights), shape[position] // shards_of).reshape((-1,) + (1,) * (len(shape) - position - 1))

    level = one(*cuts[0])
    for cut in cuts[1:]:
        level = level * one(*cut)
    return level


def setup_inputs(seed: int = 0, part: int = 0) -> dict:
    streams_of = jax.random.split(jax.random.key(seed), 9)
    part_keys = jax.random.split(jax.random.fold_in(streams_of[8], part), 9)
    start_density = jnp.clip(jnp.exp(math.log(2.0) - 2.9957323 * jax.random.uniform(part_keys[0], (CLASSES, CELLS), jnp.float32) ** shard_levels(part_keys[0], (CLASSES, CELLS), ((0, 2), (1, 4)), -0.2, 0.2)), 0.1, 2.0)
    final_value = draw_final_value(jax.random.fold_in(jax.random.fold_in(streams_of[8], part), 71), part)
    congestion = jnp.clip(jnp.exp(math.log(10.0) - 4.6051702 * jax.random.uniform(part_keys[2], (STEPS, CELLS), jnp.float32) ** shard_levels(part_keys[2], (STEPS, CELLS), ((0, 2), (1, 4)), -0.2, 0.2)), 0.1, 10.0)
    capacity = jnp.clip(jnp.exp(math.log(4.0) - 2.0794415 * jax.random.uniform(part_keys[3], (CELLS,), jnp.float32) ** shard_levels(part_keys[3], (CELLS,), ((0, 4),), -0.2, 0.2)), 0.5, 4.0)
    trans_values = jnp.clip(jnp.exp(math.log(0.0046691895) - 3.4024236 * jax.random.uniform(part_keys[4], (EDGES, BS, BS), jnp.float32) ** shard_levels(part_keys[4], (EDGES, BS, BS), ((0, 4),), -0.2, 0.2)), 0.00015544891, 0.0046691895).astype(jnp.bfloat16)
    src_local = touch_ends(jax.random.randint(part_keys[5], (EDGES,), 0, BLK_DEV), jax.random.fold_in(part_keys[5], 1), 0, BLK_DEV - 1).astype(jnp.int32)
    dst_local = touch_ends(jax.random.randint(part_keys[6], (EDGES,), 0, BLK_DEV), jax.random.fold_in(part_keys[6], 1), 0, BLK_DEV - 1).astype(jnp.int32)
    bucket_len = draw_bucket_len(jax.random.fold_in(jax.random.fold_in(streams_of[8], part), 71), part)
    return {"start_density": start_density, "final_value": final_value, "congestion": congestion, "capacity": capacity, "trans_values": trans_values, "src_local": src_local, "dst_local": dst_local, "bucket_len": bucket_len}


softness = 1.0
base_cost = 0.05
far_below = -1e30


def reference(start_density, final_value, congestion, capacity, trans_values, src_local, dst_local, bucket_len):
    blocks = BLK_DEV * N_CELLS
    edge_index = jnp.arange(EDGES, dtype=jnp.int32)
    owning = edge_index // EDGE_DEV
    slot_index = edge_index % EDGE_DEV
    peer_index = slot_index // CAP
    active_slot = (slot_index % CAP) < bucket_len[owning * N_CELLS + peer_index]
    source = (owning * BLK_DEV + src_local).astype(jnp.int32)
    target = (peer_index * BLK_DEV + dst_local).astype(jnp.int32)
    loading = congestion.reshape(STEPS, blocks, BS) / capacity.reshape(1, blocks, BS)
    mobility = 1.0 / (1.0 + loading)
    travel = base_cost * (1.0 + loading)
    kernel = trans_values.astype(jnp.float32)

    masses = start_density.reshape(CLASSES, blocks, BS)
    history = []
    for moment in range(STEPS):
        moving = (masses * mobility[moment]).astype(jnp.bfloat16)
        picked = moving[:, source].astype(jnp.float32)
        partial_value = jnp.einsum("ceb,ebk->eck", picked, kernel).astype(jnp.bfloat16)
        partial_value = jnp.where(active_slot[:, None, None], partial_value, jnp.zeros_like(partial_value))
        inflow = jax.ops.segment_sum(partial_value.astype(jnp.float32), target, num_segments=blocks)
        masses = masses * (1.0 - mobility[moment]) + jnp.transpose(inflow, (1, 0, 2))
        history.append(masses.reshape(CLASSES, blocks * BS))
    density = jnp.stack(history)
    class_mean = jnp.sum(density, axis=1) / CLASSES

    values_now = final_value.reshape(CLASSES, blocks, BS)
    backward_list = [None] * STEPS
    for moment in reversed(range(STEPS)):
        block_low = jnp.min(values_now, axis=2).astype(jnp.bfloat16)
        low_wide = lax.optimization_barrier(block_low).astype(jnp.float32)
        weight = jnp.exp(-(values_now - low_wide[:, :, None]) / softness).astype(jnp.bfloat16)
        gathered = weight[:, target].astype(jnp.float32)
        kernel_sums = jnp.einsum("eij,cej->cei", kernel, gathered)
        edge_log = jnp.where(active_slot[None, :], -low_wide[:, target] / softness, far_below)
        block_top = jax.ops.segment_max(jnp.transpose(edge_log), source, num_segments=blocks)
        stay_log = -values_now / softness
        ceiling = jnp.maximum(stay_log, jnp.transpose(block_top)[:, :, None])
        edge_terms = jnp.exp(edge_log[:, :, None] - ceiling[:, source]) * kernel_sums
        edge_total = jax.ops.segment_sum(jnp.transpose(edge_terms, (1, 0, 2)), source, num_segments=blocks)
        grand_total = jnp.exp(stay_log - ceiling) + jnp.transpose(edge_total, (1, 0, 2))
        values_now = travel[moment] - softness * (ceiling + jnp.log(grand_total))
        backward_list[moment] = values_now.reshape(CLASSES, blocks * BS)
    return density, class_mean, jnp.stack(backward_list)
```

```python
import functools

import jax
import jax.numpy as jnp
from jax import lax
from jax.experimental import pallas as pl
from jax.experimental.pallas import tpu as pltpu
from jax.sharding import PartitionSpec as P

BS = 128
CLASSES = 64

base_cost = 0.05
far_below = -1e30
MESH = pl.DeviceIdType.MESH


def loop(low, high, body, carry):
    if high - low <= 8:
        for index in range(low, high):
            carry = body(index, carry)
        return carry
    return lax.fori_loop(low, high, body, carry)


def kernel(
    sizes, src_s, dst_s, len_s, start_hbm, final_hbm, cong_hbm, cap_hbm, trans_hbm,
    dens_out, mean_out, val_out,
    masses, values, cong, cap, trans, moving, weight, ceiling, edge_log, sums,
    dst_send, dst_recv, part_send, part_recv, back_send, back_recv, class_sums,
    in_sem, dst_ssem, dst_rsem, part_ssem, part_rsem, back_ssem, back_rsem,
    cong_ssem, cong_rsem, mean_ssem, mean_rsem,
):
    owners, sections, halves, per_peer, local_steps, block_count, class_count = sizes
    steps = sections * local_steps
    me = lax.axis_index("cells")
    section = lax.axis_index("tm")
    half = lax.axis_index("cls")
    columns = [slice(b * BS, (b + 1) * BS) for b in range(block_count)]

    def after(axis, size, by):
        return {axis: lax.rem(lax.axis_index(axis) + by, size)}

    barrier = pltpu.get_barrier_semaphore()
    greeted = 0
    for axis, size in (("cells", owners), ("tm", sections), ("cls", halves)):

        def greet(by, carry, axis=axis, size=size):
            pl.semaphore_signal(
                barrier, inc=1, device_id=after(axis, size, by), device_id_type=MESH
            )
            return carry

        loop(1, size, greet, 0)
        greeted += size - 1

    own_cong = cong.at[section]
    loads = [
        pltpu.make_async_copy(cong_hbm, own_cong, in_sem.at[0]),
        pltpu.make_async_copy(cap_hbm, cap, in_sem.at[1]),
        pltpu.make_async_copy(final_hbm, values, in_sem.at[2]),
        pltpu.make_async_copy(start_hbm, masses, in_sem.at[3]),
        pltpu.make_async_copy(trans_hbm, trans, in_sem.at[4]),
    ]
    for load in loads:
        load.start()

    def target_rows(by, carry):
        peer = lax.rem(me + by, owners)
        for s in range(per_peer):
            target = jnp.where(s < len_s[peer], dst_s[peer * per_peer + s], -1)
            dst_send[by, s : s + 1, :] = jnp.full((1, BS), target, jnp.int32)
        return carry

    loop(0, owners, target_rows, 0)
    dst_recv[0] = dst_send[0]
    pl.semaphore_wait(barrier, greeted)

    def dst_copy(by):
        return pltpu.make_async_remote_copy(
            src_ref=dst_send.at[by], dst_ref=dst_recv.at[by],
            send_sem=dst_ssem.at[by], recv_sem=dst_rsem.at[by],
            device_id=after("cells", owners, by), device_id_type=MESH,
        )

    def cong_copy(by):
        return pltpu.make_async_remote_copy(
            src_ref=cong_hbm, dst_ref=cong.at[section],
            send_sem=cong_ssem.at[by], recv_sem=cong_rsem.at[section],
            device_id=after("tm", sections, by), device_id_type=MESH,
        )

    def cong_arrival(owner):
        return pltpu.make_async_remote_copy(
            src_ref=cong_hbm, dst_ref=cong.at[owner],
            send_sem=cong_ssem.at[0], recv_sem=cong_rsem.at[owner],
            device_id=after("tm", sections, 1), device_id_type=MESH,
        )

    def part_copy(r, by):
        return pltpu.make_async_remote_copy(
            src_ref=part_send.at[r, by], dst_ref=part_recv.at[r, by],
            send_sem=part_ssem.at[r, by], recv_sem=part_rsem.at[r, by],
            device_id=after("cells", owners, by), device_id_type=MESH,
        )

    def back_copy(r, by):
        return pltpu.make_async_remote_copy(
            src_ref=back_send.at[r, by], dst_ref=back_recv.at[r, by],
            send_sem=back_ssem.at[r, by], recv_sem=back_rsem.at[r, by],
            device_id=after("cells", owners, owners - by), device_id_type=MESH,
        )

    def mean_copy(by):
        return pltpu.make_async_remote_copy(
            src_ref=class_sums.at[0], dst_ref=class_sums.at[by],
            send_sem=mean_ssem.at[by], recv_sem=mean_rsem.at[by],
            device_id=after("cls", halves, by), device_id_type=MESH,
        )

    def started(copy):
        def body(by, carry):
            copy(by).start()
            return carry

        return body

    def sent(copy):
        def body(by, carry):
            copy(by).wait_send()
            return carry

        return body

    loop(1, sections, started(cong_copy), 0)
    loop(1, owners, started(dst_copy), 0)

    def one_loading(step, b):
        owner, local = divmod(step, local_steps)
        return cong[owner, local : local + 1, columns[b]] / cap[:, columns[b]]

    def forward_send(r):
        owner, local = divmod(r, local_steps)
        if owner < sections - 1 and local == 0:

            @pl.when(section > owner)
            def _():
                cong_arrival(owner).wait_recv()

        for b in range(block_count):
            mobility = 1.0 / (1.0 + one_loading(r, b))
            now = masses[:, columns[b]]
            moving[b] = (now * mobility).astype(jnp.bfloat16)
            masses[:, columns[b]] = now * (1.0 - mobility)

        def one_peer(by, carry):
            peer = lax.rem(me + by, owners)
            into = part_recv if isinstance(by, int) and by == 0 else part_send
            for s in range(per_peer):
                e = peer * per_peer + s
                into[r, by, s] = jnp.dot(
                    moving[src_s[e]], trans[e], preferred_element_type=jnp.float32
                ).astype(jnp.bfloat16)
            if into is part_send:
                part_copy(r, by).start()
            return carry

        loop(1, owners, one_peer, 0)
        one_peer(0, 0)

    def forward_receive(r):
        owner, local = divmod(r, local_steps)

        def one_source(by, totals):
            if not (isinstance(by, int) and by == 0):
                part_copy(r, by).wait_recv()
            totals = list(totals)
            for s in range(per_peer):
                row = jnp.broadcast_to(dst_recv[by, s : s + 1, :], (class_count, BS))
                part = part_recv[r, by, s].astype(jnp.float32)
                for b in range(block_count):
                    totals[b] = totals[b] + jnp.where(row == b, part, 0.0)
            return tuple(totals)

        totals = one_source(0, tuple(masses[:, c] for c in columns))
        totals = loop(1, owners, one_source, totals)
        for b in range(block_count):
            masses[:, columns[b]] = totals[b]

        @pl.when(section == owner)
        def _():
            for b in range(block_count):
                total = masses[:, columns[b]]
                dens_out[local, :, columns[b]] = total
                class_sums[0, local : local + 1, columns[b]] = jnp.sum(
                    total, axis=0, keepdims=True
                )
            if local == local_steps - 1:
                loop(1, halves, started(mean_copy), 0)

    def backward_send(r):
        lane = lax.broadcasted_iota(jnp.int32, (class_count, BS), 1)
        lows = jnp.zeros((class_count, BS), jnp.float32)
        for b in range(block_count):
            now = values[:, columns[b]]
            low = jnp.min(now, axis=1, keepdims=True)
            low = low.astype(jnp.bfloat16).astype(jnp.float32)
            weight[b] = jnp.exp(low - now)
            lows = jnp.where(lane == b, low, lows)
        lows = lows.astype(jnp.bfloat16)

        def one_source(by, carry):
            here = isinstance(by, int) and by == 0
            into = back_recv if here else back_send
            if r == 0 and not here:
                dst_copy(by).wait_recv()
            for s in range(per_peer):
                row = jnp.broadcast_to(dst_recv[by, s : s + 1, :], (class_count, BS))
                picked = jnp.zeros((class_count, BS), jnp.float32)
                for b in range(block_count):
                    picked = jnp.where(row == b, weight[b], picked)
                into[r, by, s] = picked.astype(jnp.bfloat16)
            into[r, by, per_peer] = lows
            if not here:
                back_copy(r, by).start()
            return carry

        loop(1, owners, one_source, 0)
        one_source(0, 0)

    def backward_receive(r):
        step = steps - 1 - r
        owner, local = divmod(step, local_steps)
        lane = lax.broadcasted_iota(jnp.int32, (class_count, BS), 1)

        def one_peer(by, tops):
            if not (isinstance(by, int) and by == 0):
                back_copy(r, by).wait_recv()
            peer = lax.rem(me + by, owners)
            tops = list(tops)
            lows = back_recv[r, by, per_peer].astype(jnp.float32)
            for s in range(per_peer):
                e = peer * per_peer + s
                low = jnp.sum(jnp.where(lane == dst_s[e], lows, 0.0), axis=1, keepdims=True)
                log = jnp.where(s < len_s[peer], -low, far_below)
                log = jnp.broadcast_to(log, (class_count, BS))
                edge_log[by * per_peer + s] = log
                sums[by * per_peer + s] = lax.dot_general(
                    back_recv[r, by, s], trans[e], (((1,), (1,)), ((), ())),
                    preferred_element_type=jnp.float32,
                )
                for b in range(block_count):
                    tops[b] = jnp.maximum(tops[b], jnp.where(src_s[e] == b, log, far_below))
            return tuple(tops)

        tops = one_peer(0, tuple(-values[:, c] for c in columns))
        tops = loop(1, owners, one_peer, tops)
        for b in range(block_count):
            ceiling[b] = tops[b]

        def one_total(by, totals):
            peer = lax.rem(me + by, owners)
            totals = list(totals)
            for s in range(per_peer):
                source = src_s[peer * per_peer + s]
                place = by * per_peer + s
                term = jnp.exp(edge_log[place] - ceiling[source]) * sums[place]
                for b in range(block_count):
                    totals[b] = totals[b] + jnp.where(source == b, term, 0.0)
            return tuple(totals)

        if owner > 0 and local == local_steps - 1:

            @pl.when(section < owner)
            def _():
                cong_arrival(owner).wait_recv()

        totals = tuple(jnp.exp(-values[:, columns[b]] - ceiling[b]) for b in range(block_count))
        totals = loop(0, owners, one_total, totals)
        for b in range(block_count):
            travel = base_cost * (1.0 + one_loading(step, b))
            values[:, columns[b]] = travel - (ceiling[b] + jnp.log(totals[b]))

        @pl.when(section == owner)
        def _():
            val_out[local] = values[...]

    for load in loads:
        load.wait()

    def forward_guard(r, body):
        owner = r // local_steps
        if owner == 0:
            body(r)
        else:

            @pl.when(section >= owner)
            def _():
                body(r)


    def backward_guard(r, body):
        owner = (steps - 1 - r) // local_steps
        if owner == sections - 1:
            body(r)
        else:

            @pl.when(section <= owner)
            def _():
                body(r)


    forward_guard(0, forward_send)
    backward_guard(0, backward_send)
    for r in range(steps):
        forward_guard(r, forward_receive)
        if r + 1 < steps:
            forward_guard(r + 1, forward_send)
        backward_guard(r, backward_receive)
        if r + 1 < steps:
            backward_guard(r + 1, backward_send)

    def arrived(by, carry):
        mean_copy(by).wait_recv()
        return carry

    loop(1, halves, arrived, 0)
    total = class_sums[half]
    for index in range(1, halves):
        total = total + class_sums[lax.rem(half - index + halves, halves)]
    mean_out[...] = total / CLASSES

    loop(1, sections, sent(cong_copy), 0)
    loop(1, owners, sent(dst_copy), 0)
    loop(1, halves, sent(mean_copy), 0)
    for r in range(steps):
        forward_guard(r, lambda r: loop(1, owners, sent(functools.partial(part_copy, r)), 0))
        backward_guard(r, lambda r: loop(1, owners, sent(functools.partial(back_copy, r)), 0))


def shards(
    start_density, final_value, congestion, capacity, trans_values, src_local, dst_local, bucket_len
):
    owners = lax.axis_size("cells")
    sections = lax.axis_size("tm")
    halves = lax.axis_size("cls")
    class_count, cell_count = start_density.shape
    local_steps = congestion.shape[0]
    block_count = cell_count // BS
    edge_count = src_local.shape[0]
    per_peer = edge_count // owners
    steps = sections * local_steps
    sizes = (owners, sections, halves, per_peer, local_steps, block_count, class_count)
    scalars = pl.BlockSpec(memory_space=pltpu.SMEM)
    whole = pl.BlockSpec(memory_space=pl.ANY)
    held = pl.BlockSpec(memory_space=pltpu.VMEM)
    f32, bf16 = jnp.float32, jnp.bfloat16
    tile = (class_count, BS)
    return pl.pallas_call(
        functools.partial(kernel, sizes),
        out_shape=(
            jax.ShapeDtypeStruct((local_steps, class_count, cell_count), f32),
            jax.ShapeDtypeStruct((local_steps, cell_count), f32),
            jax.ShapeDtypeStruct((local_steps, class_count, cell_count), f32),
        ),
        in_specs=[scalars] * 3 + [whole] * 5,
        out_specs=(held, held, held),
        scratch_shapes=[
            pltpu.VMEM((class_count, cell_count), f32),
            pltpu.VMEM((class_count, cell_count), f32),
            pltpu.VMEM((sections, local_steps, cell_count), f32),
            pltpu.VMEM((1, cell_count), f32),
            pltpu.VMEM((edge_count, BS, BS), bf16),
            pltpu.VMEM((block_count, *tile), bf16),
            pltpu.VMEM((block_count, *tile), f32),
            pltpu.VMEM((block_count, *tile), f32),
            pltpu.VMEM((edge_count, *tile), f32),
            pltpu.VMEM((edge_count, *tile), f32),
            pltpu.VMEM((owners, per_peer, BS), jnp.int32),
            pltpu.VMEM((owners, per_peer, BS), jnp.int32),
            pltpu.VMEM((steps, owners, per_peer, *tile), bf16),
            pltpu.VMEM((steps, owners, per_peer, *tile), bf16),
            pltpu.VMEM((steps, owners, per_peer + 1, *tile), bf16),
            pltpu.VMEM((steps, owners, per_peer + 1, *tile), bf16),
            pltpu.VMEM((halves, local_steps, cell_count), f32),
            pltpu.SemaphoreType.DMA((5,)),
            pltpu.SemaphoreType.DMA((owners,)),
            pltpu.SemaphoreType.DMA((owners,)),
            pltpu.SemaphoreType.DMA((steps, owners)),
            pltpu.SemaphoreType.DMA((steps, owners)),
            pltpu.SemaphoreType.DMA((steps, owners)),
            pltpu.SemaphoreType.DMA((steps, owners)),
            pltpu.SemaphoreType.DMA((sections,)),
            pltpu.SemaphoreType.DMA((sections,)),
            pltpu.SemaphoreType.DMA((halves,)),
            pltpu.SemaphoreType.DMA((halves,)),
        ],
        compiler_params=pltpu.CompilerParams(
            collective_id=0, has_side_effects=True, vmem_limit_bytes=40 * 1024 * 1024
        ),
    )(
        src_local, dst_local, bucket_len, start_density, final_value, congestion,
        capacity.reshape(1, cell_count), trans_values,
    )


def solution(mesh):
    in_specs = (
        P(("groups", "cls"), "cells"),
        P(("groups", "cls"), "cells"),
        P(("groups", "tm"), "cells"),
        P(("groups", "cells")),
        P(("groups", "cells"), None, None),
        P(("groups", "cells")),
        P(("groups", "cells")),
        P(("groups", "cells")),
    )
    out_specs = (
        P(("groups", "tm"), "cls", "cells"),
        P(("groups", "tm"), "cells"),
        P(("groups", "tm"), "cls", "cells"),
    )
    return jax.shard_map(shards, mesh=mesh, in_specs=in_specs, out_specs=out_specs, check_vma=False)
```

```python
import functools

import jax
import jax.numpy as jnp
from jax import lax
from jax.experimental import pallas as pl
from jax.experimental.pallas import tpu as pltpu
from jax.sharding import PartitionSpec as P

BS = 128
CLASSES = 64

base_cost = 0.05
far_below = -1e30
VMEM_BYTES = 64 * 1024 * 1024
VMEM_SPARE = 256 * 1024
MESH = pl.DeviceIdType.MESH


def loop(low, high, body, carry):
    if high - low <= 8:
        for index in range(low, high):
            carry = body(index, carry)
        return carry
    return lax.fori_loop(low, high, body, carry)


def kernel(
    sizes, src_hbm, dst_hbm, len_hbm, start_hbm, final_hbm, cong_hbm, cap_hbm, trans_hbm,
    dens_hbm, mean_hbm, val_hbm,
    dens_out, mean_out, val_out, out_sem, src_s, dst_s, len_s,
    masses, values, cong, cap, trans, moving, weight, ceiling, edge_log, sums,
    dst_send, dst_recv, part_send, part_recv, back_send, back_recv, class_sums,
    in_sem, dst_ssem, dst_rsem, part_ssem, part_rsem, back_ssem, back_rsem,
    cong_ssem, cong_rsem, mean_ssem, mean_rsem,
):
    owners, sections, halves, per_peer, local_steps, block_count, class_count = sizes
    steps = sections * local_steps
    me = lax.axis_index("cells")
    section = lax.axis_index("tm")
    half = lax.axis_index("cls")
    columns = [slice(b * BS, (b + 1) * BS) for b in range(block_count)]

    def after(axis, size, by):
        return {axis: lax.rem(lax.axis_index(axis) + by, size)}

    barrier = pltpu.get_barrier_semaphore()
    greeted = 0
    for axis, size in (("cells", owners), ("tm", sections), ("cls", halves)):

        def greet(by, carry, axis=axis, size=size):
            pl.semaphore_signal(
                barrier, inc=1, device_id=after(axis, size, by), device_id_type=MESH
            )
            return carry

        loop(1, size, greet, 0)
        greeted += size - 1

    dens_store = pltpu.make_async_copy(dens_out, dens_hbm, out_sem.at[0])
    val_store = pltpu.make_async_copy(val_out, val_hbm, out_sem.at[1])
    mean_store = pltpu.make_async_copy(mean_out, mean_hbm, out_sem.at[2])
    own_cong = cong.at[section]
    scalar_loads = [
        pltpu.make_async_copy(src_hbm, src_s, in_sem.at[5]),
        pltpu.make_async_copy(dst_hbm, dst_s, in_sem.at[6]),
        pltpu.make_async_copy(len_hbm, len_s, in_sem.at[7]),
    ]
    loads = [
        pltpu.make_async_copy(cong_hbm, own_cong, in_sem.at[0]),
        pltpu.make_async_copy(cap_hbm, cap, in_sem.at[1]),
        pltpu.make_async_copy(final_hbm, values, in_sem.at[2]),
        pltpu.make_async_copy(start_hbm, masses, in_sem.at[3]),
        pltpu.make_async_copy(trans_hbm, trans, in_sem.at[4]),
    ]
    for load in scalar_loads + loads:
        load.start()
    for load in scalar_loads:
        load.wait()

    def target_rows(by, carry):
        peer = lax.rem(me + by, owners)
        for s in range(per_peer):
            target = jnp.where(s < len_s[peer], dst_s[peer * per_peer + s], -1)
            dst_send[by, s : s + 1, :] = jnp.full((1, BS), target, jnp.int32)
        return carry

    loop(0, owners, target_rows, 0)
    dst_recv[0] = dst_send[0]
    pl.semaphore_wait(barrier, greeted)

    def dst_copy(by):
        return pltpu.make_async_remote_copy(
            src_ref=dst_send.at[by], dst_ref=dst_recv.at[by],
            send_sem=dst_ssem.at[by], recv_sem=dst_rsem.at[by],
            device_id=after("cells", owners, by), device_id_type=MESH,
        )

    def cong_copy(by):
        return pltpu.make_async_remote_copy(
            src_ref=cong_hbm, dst_ref=cong.at[section],
            send_sem=cong_ssem.at[by], recv_sem=cong_rsem.at[section],
            device_id=after("tm", sections, by), device_id_type=MESH,
        )

    def cong_arrival(owner):
        return pltpu.make_async_remote_copy(
            src_ref=cong_hbm, dst_ref=cong.at[owner],
            send_sem=cong_ssem.at[0], recv_sem=cong_rsem.at[owner],
            device_id=after("tm", sections, 1), device_id_type=MESH,
        )

    def part_copy(r, by):
        return pltpu.make_async_remote_copy(
            src_ref=part_send.at[r, by], dst_ref=part_recv.at[r, by],
            send_sem=part_ssem.at[r, by], recv_sem=part_rsem.at[r, by],
            device_id=after("cells", owners, by), device_id_type=MESH,
        )

    def back_copy(r, by):
        return pltpu.make_async_remote_copy(
            src_ref=back_send.at[r, by], dst_ref=back_recv.at[r, by],
            send_sem=back_ssem.at[r, by], recv_sem=back_rsem.at[r, by],
            device_id=after("cells", owners, owners - by), device_id_type=MESH,
        )

    def mean_copy(by):
        return pltpu.make_async_remote_copy(
            src_ref=class_sums.at[0], dst_ref=class_sums.at[by],
            send_sem=mean_ssem.at[by], recv_sem=mean_rsem.at[by],
            device_id=after("cls", halves, by), device_id_type=MESH,
        )

    def started(copy):
        def body(by, carry):
            copy(by).start()
            return carry

        return body

    def sent(copy):
        def body(by, carry):
            copy(by).wait_send()
            return carry

        return body

    loop(1, sections, started(cong_copy), 0)
    loop(1, owners, started(dst_copy), 0)

    def one_loading(step, b):
        owner, local = divmod(step, local_steps)
        return cong[owner, local : local + 1, columns[b]] / cap[:, columns[b]]

    def forward_send(r):
        owner, local = divmod(r, local_steps)
        if owner < sections - 1 and local == 0:

            @pl.when(section > owner)
            def _():
                cong_arrival(owner).wait_recv()

        for b in range(block_count):
            mobility = 1.0 / (1.0 + one_loading(r, b))
            now = masses[:, columns[b]]
            moving[b] = (now * mobility).astype(jnp.bfloat16)
            masses[:, columns[b]] = now * (1.0 - mobility)

        def one_peer(by, carry):
            peer = lax.rem(me + by, owners)
            into = part_recv if isinstance(by, int) and by == 0 else part_send
            for s in range(per_peer):
                e = peer * per_peer + s
                into[r, by, s] = jnp.dot(
                    moving[src_s[e]], trans[e], preferred_element_type=jnp.float32
                ).astype(jnp.bfloat16)
            if into is part_send:
                part_copy(r, by).start()
            return carry

        loop(1, owners, one_peer, 0)
        one_peer(0, 0)

    def forward_receive(r):
        owner, local = divmod(r, local_steps)

        def one_source(by, totals):
            if not (isinstance(by, int) and by == 0):
                part_copy(r, by).wait_recv()
            totals = list(totals)
            for s in range(per_peer):
                row = jnp.broadcast_to(dst_recv[by, s : s + 1, :], (class_count, BS))
                part = part_recv[r, by, s].astype(jnp.float32)
                for b in range(block_count):
                    totals[b] = totals[b] + jnp.where(row == b, part, 0.0)
            return tuple(totals)

        totals = one_source(0, tuple(masses[:, c] for c in columns))
        totals = loop(1, owners, one_source, totals)
        for b in range(block_count):
            masses[:, columns[b]] = totals[b]

        @pl.when(section == owner)
        def _():
            for b in range(block_count):
                total = masses[:, columns[b]]
                dens_out[local, :, columns[b]] = total
                class_sums[0, local : local + 1, columns[b]] = jnp.sum(
                    total, axis=0, keepdims=True
                )
            if local == local_steps - 1:
                loop(1, halves, started(mean_copy), 0)
                dens_store.start()

    def backward_send(r):
        lane = lax.broadcasted_iota(jnp.int32, (class_count, BS), 1)
        lows = jnp.zeros((class_count, BS), jnp.float32)
        for b in range(block_count):
            now = values[:, columns[b]]
            low = jnp.min(now, axis=1, keepdims=True)
            low = low.astype(jnp.bfloat16).astype(jnp.float32)
            weight[b] = jnp.exp(low - now)
            lows = jnp.where(lane == b, low, lows)
        lows = lows.astype(jnp.bfloat16)

        def one_source(by, carry):
            here = isinstance(by, int) and by == 0
            into = back_recv if here else back_send
            if r == 0 and not here:
                dst_copy(by).wait_recv()
            for s in range(per_peer):
                row = jnp.broadcast_to(dst_recv[by, s : s + 1, :], (class_count, BS))
                picked = jnp.zeros((class_count, BS), jnp.float32)
                for b in range(block_count):
                    picked = jnp.where(row == b, weight[b], picked)
                into[r, by, s] = picked.astype(jnp.bfloat16)
            into[r, by, per_peer] = lows
            if not here:
                back_copy(r, by).start()
            return carry

        loop(1, owners, one_source, 0)
        one_source(0, 0)

    def backward_receive(r):
        step = steps - 1 - r
        owner, local = divmod(step, local_steps)
        lane = lax.broadcasted_iota(jnp.int32, (class_count, BS), 1)

        def one_peer(by, tops):
            if not (isinstance(by, int) and by == 0):
                back_copy(r, by).wait_recv()
            peer = lax.rem(me + by, owners)
            tops = list(tops)
            lows = back_recv[r, by, per_peer].astype(jnp.float32)
            for s in range(per_peer):
                e = peer * per_peer + s
                low = jnp.sum(jnp.where(lane == dst_s[e], lows, 0.0), axis=1, keepdims=True)
                log = jnp.where(s < len_s[peer], -low, far_below)
                log = jnp.broadcast_to(log, (class_count, BS))
                edge_log[by * per_peer + s] = log
                sums[by * per_peer + s] = lax.dot_general(
                    back_recv[r, by, s], trans[e], (((1,), (1,)), ((), ())),
                    preferred_element_type=jnp.float32,
                )
                for b in range(block_count):
                    tops[b] = jnp.maximum(tops[b], jnp.where(src_s[e] == b, log, far_below))
            return tuple(tops)

        tops = one_peer(0, tuple(-values[:, c] for c in columns))
        tops = loop(1, owners, one_peer, tops)
        for b in range(block_count):
            ceiling[b] = tops[b]

        def one_total(by, totals):
            peer = lax.rem(me + by, owners)
            totals = list(totals)
            for s in range(per_peer):
                source = src_s[peer * per_peer + s]
                place = by * per_peer + s
                term = jnp.exp(edge_log[place] - ceiling[source]) * sums[place]
                for b in range(block_count):
                    totals[b] = totals[b] + jnp.where(source == b, term, 0.0)
            return tuple(totals)

        if owner > 0 and local == local_steps - 1:

            @pl.when(section < owner)
            def _():
                cong_arrival(owner).wait_recv()

        totals = tuple(jnp.exp(-values[:, columns[b]] - ceiling[b]) for b in range(block_count))
        totals = loop(0, owners, one_total, totals)
        for b in range(block_count):
            travel = base_cost * (1.0 + one_loading(step, b))
            values[:, columns[b]] = travel - (ceiling[b] + jnp.log(totals[b]))

        @pl.when(section == owner)
        def _():
            for b in range(block_count):
                val_out[local, :, columns[b]] = values[:, columns[b]]
            if local == 0:
                val_store.start()

    for load in loads:
        load.wait()

    def forward_guard(r, body):
        owner = r // local_steps
        if owner == 0:
            body(r)
        else:

            @pl.when(section >= owner)
            def _():
                body(r)


    def backward_guard(r, body):
        owner = (steps - 1 - r) // local_steps
        if owner == sections - 1:
            body(r)
        else:

            @pl.when(section <= owner)
            def _():
                body(r)


    forward_guard(0, forward_send)
    backward_guard(0, backward_send)
    for r in range(steps):
        forward_guard(r, forward_receive)
        if r + 1 < steps:
            forward_guard(r + 1, forward_send)
        backward_guard(r, backward_receive)
        if r + 1 < steps:
            backward_guard(r + 1, backward_send)

    def arrived(by, carry):
        mean_copy(by).wait_recv()
        return carry

    loop(1, halves, arrived, 0)
    total = class_sums[half]
    for index in range(1, halves):
        total = total + class_sums[lax.rem(half - index + halves, halves)]
    mean_out[...] = total / CLASSES
    mean_store.start()

    loop(1, sections, sent(cong_copy), 0)
    loop(1, owners, sent(dst_copy), 0)
    loop(1, halves, sent(mean_copy), 0)
    for r in range(steps):
        forward_guard(r, lambda r: loop(1, owners, sent(functools.partial(part_copy, r)), 0))
        backward_guard(r, lambda r: loop(1, owners, sent(functools.partial(back_copy, r)), 0))
    dens_store.wait()
    val_store.wait()
    mean_store.wait()


def write_out(dens_in, mean_in, val_in, dens_out, mean_out, val_out, sem):
    copies = [
        pltpu.make_async_copy(dens_in, dens_out, sem.at[0]),
        pltpu.make_async_copy(val_in, val_out, sem.at[1]),
        pltpu.make_async_copy(mean_in, mean_out, sem.at[2]),
    ]
    for copy in copies:
        copy.start()
    for copy in copies:
        copy.wait()


def shards(
    start_density, final_value, congestion, capacity, trans_values, src_local, dst_local, bucket_len
):
    owners = lax.axis_size("cells")
    sections = lax.axis_size("tm")
    halves = lax.axis_size("cls")
    class_count, cell_count = start_density.shape
    local_steps = congestion.shape[0]
    block_count = cell_count // BS
    edge_count = src_local.shape[0]
    per_peer = edge_count // owners
    steps = sections * local_steps
    sizes = (owners, sections, halves, per_peer, local_steps, block_count, class_count)
    far = pl.BlockSpec(memory_space=pltpu.HBM)
    whole = pl.BlockSpec(memory_space=pl.ANY)
    f32, bf16 = jnp.float32, jnp.bfloat16
    tile = (class_count, BS)
    results = (
        jax.ShapeDtypeStruct((local_steps, class_count, cell_count), f32),
        jax.ShapeDtypeStruct((local_steps, cell_count), f32),
        jax.ShapeDtypeStruct((local_steps, class_count, cell_count), f32),
    )
    computed = pl.pallas_call(
        functools.partial(kernel, sizes),
        out_shape=results,
        in_specs=[far] * 8,
        out_specs=(whole, whole, whole),
        scratch_shapes=[
            pltpu.VMEM((local_steps, class_count, cell_count), f32),
            pltpu.VMEM((local_steps, cell_count), f32),
            pltpu.VMEM((local_steps, class_count, cell_count), f32),
            pltpu.SemaphoreType.DMA((3,)),
            pltpu.SMEM((edge_count,), jnp.int32),
            pltpu.SMEM((edge_count,), jnp.int32),
            pltpu.SMEM((owners,), jnp.int32),
            pltpu.VMEM((class_count, cell_count), f32),
            pltpu.VMEM((class_count, cell_count), f32),
            pltpu.VMEM((sections, local_steps, cell_count), f32),
            pltpu.VMEM((1, cell_count), f32),
            pltpu.VMEM((edge_count, BS, BS), bf16),
            pltpu.VMEM((block_count, *tile), bf16),
            pltpu.VMEM((block_count, *tile), f32),
            pltpu.VMEM((block_count, *tile), f32),
            pltpu.VMEM((edge_count, *tile), f32),
            pltpu.VMEM((edge_count, *tile), f32),
            pltpu.VMEM((owners, per_peer, BS), jnp.int32),
            pltpu.VMEM((owners, per_peer, BS), jnp.int32),
            pltpu.VMEM((steps, owners, per_peer, *tile), bf16),
            pltpu.VMEM((steps, owners, per_peer, *tile), bf16),
            pltpu.VMEM((steps, owners, per_peer + 1, *tile), bf16),
            pltpu.VMEM((steps, owners, per_peer + 1, *tile), bf16),
            pltpu.VMEM((halves, local_steps, cell_count), f32),
            pltpu.SemaphoreType.DMA((8,)),
            pltpu.SemaphoreType.DMA((owners,)),
            pltpu.SemaphoreType.DMA((owners,)),
            pltpu.SemaphoreType.DMA((steps, owners)),
            pltpu.SemaphoreType.DMA((steps, owners)),
            pltpu.SemaphoreType.DMA((steps, owners)),
            pltpu.SemaphoreType.DMA((steps, owners)),
            pltpu.SemaphoreType.DMA((sections,)),
            pltpu.SemaphoreType.DMA((sections,)),
            pltpu.SemaphoreType.DMA((halves,)),
            pltpu.SemaphoreType.DMA((halves,)),
        ],
        compiler_params=pltpu.CompilerParams(
            collective_id=0, has_side_effects=True, vmem_limit_bytes=VMEM_BYTES - VMEM_SPARE
        ),
    )(
        src_local, dst_local, bucket_len, start_density, final_value, congestion,
        capacity.reshape(1, cell_count), trans_values,
    )
    return pl.pallas_call(
        write_out,
        out_shape=results,
        in_specs=[whole] * 3,
        out_specs=[whole] * 3,
        scratch_shapes=[pltpu.SemaphoreType.DMA((3,))],
        compiler_params=pltpu.CompilerParams(vmem_limit_bytes=VMEM_BYTES - VMEM_SPARE),
    )(*computed)


def solution(mesh):
    in_specs = (
        P(("groups", "cls"), "cells"),
        P(("groups", "cls"), "cells"),
        P(("groups", "tm"), "cells"),
        P(("groups", "cells")),
        P(("groups", "cells"), None, None),
        P(("groups", "cells")),
        P(("groups", "cells")),
        P(("groups", "cells")),
    )
    out_specs = (
        P(("groups", "tm"), "cls", "cells"),
        P(("groups", "tm"), "cells"),
        P(("groups", "tm"), "cls", "cells"),
    )
    return jax.shard_map(shards, mesh=mesh, in_specs=in_specs, out_specs=out_specs, check_vma=False)
```

```python
import functools

import jax
import jax.numpy as jnp
from jax import lax
from jax.experimental import pallas as pl
from jax.experimental.pallas import tpu as pltpu
from jax.sharding import PartitionSpec as P

BS = 128
CLASSES = 64

base_cost = 0.05
far_below = -1e30
KERNEL_BYTES = 32 * 1024 * 1024
MESH = pl.DeviceIdType.MESH


def loop(low, high, body, carry):
    if high - low <= 8:
        for index in range(low, high):
            carry = body(index, carry)
        return carry
    return lax.fori_loop(low, high, body, carry)


def kernel(
    sizes, src_hbm, dst_hbm, len_hbm, start_hbm, final_hbm, cong_hbm, cap_hbm, trans_hbm,
    dens_out, mean_out, val_out,
    src_s, dst_s, len_s,
    masses, values, cong, cap, trans, moving, weight, ceiling, edge_log, sums,
    dst_send, dst_recv, part_send, part_recv, back_send, back_recv, class_sums,
    in_sem, dst_ssem, dst_rsem, part_ssem, part_rsem, back_ssem, back_rsem,
    cong_ssem, cong_rsem, mean_ssem, mean_rsem,
):
    owners, sections, halves, per_peer, local_steps, block_count, class_count = sizes
    steps = sections * local_steps
    me = lax.axis_index("cells")
    section = lax.axis_index("tm")
    half = lax.axis_index("cls")
    columns = [slice(b * BS, (b + 1) * BS) for b in range(block_count)]

    def after(axis, size, by):
        return {axis: lax.rem(lax.axis_index(axis) + by, size)}

    barrier = pltpu.get_barrier_semaphore()
    greeted = 0
    for axis, size in (("cells", owners), ("tm", sections), ("cls", halves)):

        def greet(by, carry, axis=axis, size=size):
            pl.semaphore_signal(
                barrier, inc=1, device_id=after(axis, size, by), device_id_type=MESH
            )
            return carry

        loop(1, size, greet, 0)
        greeted += size - 1

    own_cong = cong.at[section]
    scalar_loads = [
        pltpu.make_async_copy(src_hbm, src_s, in_sem.at[5]),
        pltpu.make_async_copy(dst_hbm, dst_s, in_sem.at[6]),
        pltpu.make_async_copy(len_hbm, len_s, in_sem.at[7]),
    ]
    loads = [
        pltpu.make_async_copy(cong_hbm, own_cong, in_sem.at[0]),
        pltpu.make_async_copy(cap_hbm, cap, in_sem.at[1]),
        pltpu.make_async_copy(final_hbm, values, in_sem.at[2]),
        pltpu.make_async_copy(start_hbm, masses, in_sem.at[3]),
        pltpu.make_async_copy(trans_hbm, trans, in_sem.at[4]),
    ]
    for load in scalar_loads + loads:
        load.start()
    for load in scalar_loads:
        load.wait()

    def target_rows(by, carry):
        peer = lax.rem(me + by, owners)
        for s in range(per_peer):
            target = jnp.where(s < len_s[peer], dst_s[peer * per_peer + s], -1)
            dst_send[by, s : s + 1, :] = jnp.full((1, BS), target, jnp.int32)
        return carry

    loop(0, owners, target_rows, 0)
    dst_recv[0] = dst_send[0]
    pl.semaphore_wait(barrier, greeted)

    def dst_copy(by):
        return pltpu.make_async_remote_copy(
            src_ref=dst_send.at[by], dst_ref=dst_recv.at[by],
            send_sem=dst_ssem.at[by], recv_sem=dst_rsem.at[by],
            device_id=after("cells", owners, by), device_id_type=MESH,
        )

    def cong_copy(by):
        return pltpu.make_async_remote_copy(
            src_ref=cong_hbm, dst_ref=cong.at[section],
            send_sem=cong_ssem.at[by], recv_sem=cong_rsem.at[section],
            device_id=after("tm", sections, by), device_id_type=MESH,
        )

    def cong_arrival(owner):
        return pltpu.make_async_remote_copy(
            src_ref=cong_hbm, dst_ref=cong.at[owner],
            send_sem=cong_ssem.at[0], recv_sem=cong_rsem.at[owner],
            device_id=after("tm", sections, 1), device_id_type=MESH,
        )

    def part_copy(r, by):
        return pltpu.make_async_remote_copy(
            src_ref=part_send.at[r, by], dst_ref=part_recv.at[r, by],
            send_sem=part_ssem.at[r, by], recv_sem=part_rsem.at[r, by],
            device_id=after("cells", owners, by), device_id_type=MESH,
        )

    def back_copy(r, by):
        return pltpu.make_async_remote_copy(
            src_ref=back_send.at[r, by], dst_ref=back_recv.at[r, by],
            send_sem=back_ssem.at[r, by], recv_sem=back_rsem.at[r, by],
            device_id=after("cells", owners, owners - by), device_id_type=MESH,
        )

    def mean_copy(by):
        return pltpu.make_async_remote_copy(
            src_ref=class_sums.at[0], dst_ref=class_sums.at[by],
            send_sem=mean_ssem.at[by], recv_sem=mean_rsem.at[by],
            device_id=after("cls", halves, by), device_id_type=MESH,
        )

    def started(copy):
        def body(by, carry):
            copy(by).start()
            return carry

        return body

    def sent(copy):
        def body(by, carry):
            copy(by).wait_send()
            return carry

        return body

    loop(1, sections, started(cong_copy), 0)
    loop(1, owners, started(dst_copy), 0)

    def one_loading(step, b):
        owner, local = divmod(step, local_steps)
        return cong[owner, local : local + 1, columns[b]] / cap[:, columns[b]]

    def forward_send(r):
        owner, local = divmod(r, local_steps)
        if owner < sections - 1 and local == 0:

            @pl.when(section > owner)
            def _():
                cong_arrival(owner).wait_recv()

        for b in range(block_count):
            mobility = 1.0 / (1.0 + one_loading(r, b))
            now = masses[:, columns[b]]
            moving[b] = (now * mobility).astype(jnp.bfloat16)
            masses[:, columns[b]] = now * (1.0 - mobility)

        def one_peer(by, carry):
            peer = lax.rem(me + by, owners)
            into = part_recv if isinstance(by, int) and by == 0 else part_send
            for s in range(per_peer):
                e = peer * per_peer + s
                into[r, by, s] = jnp.dot(
                    moving[src_s[e]], trans[e], preferred_element_type=jnp.float32
                ).astype(jnp.bfloat16)
            if into is part_send:
                part_copy(r, by).start()
            return carry

        loop(1, owners, one_peer, 0)
        one_peer(0, 0)

    def forward_receive(r):
        owner, local = divmod(r, local_steps)

        def one_source(by, totals):
            if not (isinstance(by, int) and by == 0):
                part_copy(r, by).wait_recv()
            totals = list(totals)
            for s in range(per_peer):
                row = jnp.broadcast_to(dst_recv[by, s : s + 1, :], (class_count, BS))
                part = part_recv[r, by, s].astype(jnp.float32)
                for b in range(block_count):
                    totals[b] = totals[b] + jnp.where(row == b, part, 0.0)
            return tuple(totals)

        totals = one_source(0, tuple(masses[:, c] for c in columns))
        totals = loop(1, owners, one_source, totals)
        for b in range(block_count):
            masses[:, columns[b]] = totals[b]

        @pl.when(section == owner)
        def _():
            for b in range(block_count):
                total = masses[:, columns[b]]
                dens_out[local, :, columns[b]] = total
                class_sums[0, local : local + 1, columns[b]] = jnp.sum(
                    total, axis=0, keepdims=True
                )
            if local == local_steps - 1:
                loop(1, halves, started(mean_copy), 0)

    def backward_send(r):
        lane = lax.broadcasted_iota(jnp.int32, (class_count, BS), 1)
        lows = jnp.zeros((class_count, BS), jnp.float32)
        for b in range(block_count):
            now = values[:, columns[b]]
            low = jnp.min(now, axis=1, keepdims=True)
            low = low.astype(jnp.bfloat16).astype(jnp.float32)
            weight[b] = jnp.exp(low - now)
            lows = jnp.where(lane == b, low, lows)
        lows = lows.astype(jnp.bfloat16)

        def one_source(by, carry):
            here = isinstance(by, int) and by == 0
            into = back_recv if here else back_send
            if r == 0 and not here:
                dst_copy(by).wait_recv()
            for s in range(per_peer):
                row = jnp.broadcast_to(dst_recv[by, s : s + 1, :], (class_count, BS))
                picked = jnp.zeros((class_count, BS), jnp.float32)
                for b in range(block_count):
                    picked = jnp.where(row == b, weight[b], picked)
                into[r, by, s] = picked.astype(jnp.bfloat16)
            into[r, by, per_peer] = lows
            if not here:
                back_copy(r, by).start()
            return carry

        loop(1, owners, one_source, 0)
        one_source(0, 0)

    def backward_receive(r):
        step = steps - 1 - r
        owner, local = divmod(step, local_steps)
        lane = lax.broadcasted_iota(jnp.int32, (class_count, BS), 1)

        def one_peer(by, tops):
            if not (isinstance(by, int) and by == 0):
                back_copy(r, by).wait_recv()
            peer = lax.rem(me + by, owners)
            tops = list(tops)
            lows = back_recv[r, by, per_peer].astype(jnp.float32)
            for s in range(per_peer):
                e = peer * per_peer + s
                low = jnp.sum(jnp.where(lane == dst_s[e], lows, 0.0), axis=1, keepdims=True)
                log = jnp.where(s < len_s[peer], -low, far_below)
                log = jnp.broadcast_to(log, (class_count, BS))
                edge_log[by * per_peer + s] = log
                sums[by * per_peer + s] = lax.dot_general(
                    back_recv[r, by, s], trans[e], (((1,), (1,)), ((), ())),
                    preferred_element_type=jnp.float32,
                )
                for b in range(block_count):
                    tops[b] = jnp.maximum(tops[b], jnp.where(src_s[e] == b, log, far_below))
            return tuple(tops)

        tops = one_peer(0, tuple(-values[:, c] for c in columns))
        tops = loop(1, owners, one_peer, tops)
        for b in range(block_count):
            ceiling[b] = tops[b]

        def one_total(by, totals):
            peer = lax.rem(me + by, owners)
            totals = list(totals)
            for s in range(per_peer):
                source = src_s[peer * per_peer + s]
                place = by * per_peer + s
                term = jnp.exp(edge_log[place] - ceiling[source]) * sums[place]
                for b in range(block_count):
                    totals[b] = totals[b] + jnp.where(source == b, term, 0.0)
            return tuple(totals)

        if owner > 0 and local == local_steps - 1:

            @pl.when(section < owner)
            def _():
                cong_arrival(owner).wait_recv()

        totals = tuple(jnp.exp(-values[:, columns[b]] - ceiling[b]) for b in range(block_count))
        totals = loop(0, owners, one_total, totals)
        for b in range(block_count):
            travel = base_cost * (1.0 + one_loading(step, b))
            values[:, columns[b]] = travel - (ceiling[b] + jnp.log(totals[b]))

        @pl.when(section == owner)
        def _():
            for b in range(block_count):
                val_out[local, :, columns[b]] = values[:, columns[b]]

    for load in loads:
        load.wait()

    def forward_guard(r, body):
        owner = r // local_steps
        if owner == 0:
            body(r)
        else:

            @pl.when(section >= owner)
            def _():
                body(r)


    def backward_guard(r, body):
        owner = (steps - 1 - r) // local_steps
        if owner == sections - 1:
            body(r)
        else:

            @pl.when(section <= owner)
            def _():
                body(r)


    forward_guard(0, forward_send)
    backward_guard(0, backward_send)
    for r in range(steps):
        forward_guard(r, forward_receive)
        if r + 1 < steps:
            forward_guard(r + 1, forward_send)
        backward_guard(r, backward_receive)
        if r + 1 < steps:
            backward_guard(r + 1, backward_send)

    def arrived(by, carry):
        mean_copy(by).wait_recv()
        return carry

    loop(1, halves, arrived, 0)
    total = class_sums[half]
    for index in range(1, halves):
        total = total + class_sums[lax.rem(half - index + halves, halves)]
    mean_out[...] = total / CLASSES

    loop(1, sections, sent(cong_copy), 0)
    loop(1, owners, sent(dst_copy), 0)
    loop(1, halves, sent(mean_copy), 0)
    for r in range(steps):
        forward_guard(r, lambda r: loop(1, owners, sent(functools.partial(part_copy, r)), 0))
        backward_guard(r, lambda r: loop(1, owners, sent(functools.partial(back_copy, r)), 0))


def write_out(dens_in, mean_in, val_in, dens_out, mean_out, val_out, sem):
    copies = [
        pltpu.make_async_copy(dens_in, dens_out, sem.at[0]),
        pltpu.make_async_copy(val_in, val_out, sem.at[1]),
        pltpu.make_async_copy(mean_in, mean_out, sem.at[2]),
    ]
    for copy in copies:
        copy.start()
    for copy in copies:
        copy.wait()


def shards(
    start_density, final_value, congestion, capacity, trans_values, src_local, dst_local, bucket_len
):
    owners = lax.axis_size("cells")
    sections = lax.axis_size("tm")
    halves = lax.axis_size("cls")
    class_count, cell_count = start_density.shape
    local_steps = congestion.shape[0]
    block_count = cell_count // BS
    edge_count = src_local.shape[0]
    per_peer = edge_count // owners
    steps = sections * local_steps
    sizes = (owners, sections, halves, per_peer, local_steps, block_count, class_count)
    held = pl.BlockSpec(memory_space=pltpu.VMEM)
    far = pl.BlockSpec(memory_space=pltpu.HBM)
    whole = pl.BlockSpec(memory_space=pl.ANY)
    f32, bf16 = jnp.float32, jnp.bfloat16
    tile = (class_count, BS)
    results = (
        jax.ShapeDtypeStruct((local_steps, class_count, cell_count), f32),
        jax.ShapeDtypeStruct((local_steps, cell_count), f32),
        jax.ShapeDtypeStruct((local_steps, class_count, cell_count), f32),
    )
    computed = pl.pallas_call(
        functools.partial(kernel, sizes),
        out_shape=tuple(pltpu.VMEM(r.shape, r.dtype) for r in results),
        in_specs=[far] * 8,
        out_specs=(held, held, held),
        scratch_shapes=[
            pltpu.SMEM((edge_count,), jnp.int32),
            pltpu.SMEM((edge_count,), jnp.int32),
            pltpu.SMEM((owners,), jnp.int32),
            pltpu.VMEM((class_count, cell_count), f32),
            pltpu.VMEM((class_count, cell_count), f32),
            pltpu.VMEM((sections, local_steps, cell_count), f32),
            pltpu.VMEM((1, cell_count), f32),
            pltpu.VMEM((edge_count, BS, BS), bf16),
            pltpu.VMEM((block_count, *tile), bf16),
            pltpu.VMEM((block_count, *tile), f32),
            pltpu.VMEM((block_count, *tile), f32),
            pltpu.VMEM((edge_count, *tile), f32),
            pltpu.VMEM((edge_count, *tile), f32),
            pltpu.VMEM((owners, per_peer, BS), jnp.int32),
            pltpu.VMEM((owners, per_peer, BS), jnp.int32),
            pltpu.VMEM((steps, owners, per_peer, *tile), bf16),
            pltpu.VMEM((steps, owners, per_peer, *tile), bf16),
            pltpu.VMEM((steps, owners, per_peer + 1, *tile), bf16),
            pltpu.VMEM((steps, owners, per_peer + 1, *tile), bf16),
            pltpu.VMEM((halves, local_steps, cell_count), f32),
            pltpu.SemaphoreType.DMA((8,)),
            pltpu.SemaphoreType.DMA((owners,)),
            pltpu.SemaphoreType.DMA((owners,)),
            pltpu.SemaphoreType.DMA((steps, owners)),
            pltpu.SemaphoreType.DMA((steps, owners)),
            pltpu.SemaphoreType.DMA((steps, owners)),
            pltpu.SemaphoreType.DMA((steps, owners)),
            pltpu.SemaphoreType.DMA((sections,)),
            pltpu.SemaphoreType.DMA((sections,)),
            pltpu.SemaphoreType.DMA((halves,)),
            pltpu.SemaphoreType.DMA((halves,)),
        ],
        compiler_params=pltpu.CompilerParams(
            collective_id=0, has_side_effects=True, vmem_limit_bytes=KERNEL_BYTES
        ),
    )(*(
        pltpu.with_memory_space_constraint(operand, pltpu.HBM)
        for operand in (
            src_local, dst_local, bucket_len, start_density, final_value, congestion,
            capacity.reshape(1, cell_count), trans_values,
        )
    ))
    return pl.pallas_call(
        write_out,
        out_shape=results,
        in_specs=[whole] * 3,
        out_specs=[whole] * 3,
        scratch_shapes=[pltpu.SemaphoreType.DMA((3,))],
    )(*computed)


def solution(mesh):
    in_specs = (
        P(("groups", "cls"), "cells"),
        P(("groups", "cls"), "cells"),
        P(("groups", "tm"), "cells"),
        P(("groups", "cells")),
        P(("groups", "cells"), None, None),
        P(("groups", "cells")),
        P(("groups", "cells")),
        P(("groups", "cells")),
    )
    out_specs = (
        P(("groups", "tm"), "cls", "cells"),
        P(("groups", "tm"), "cells"),
        P(("groups", "tm"), "cls", "cells"),
    )
    return jax.shard_map(shards, mesh=mesh, in_specs=in_specs, out_specs=out_specs, check_vma=False)
```

```python
import functools

import jax
import jax.numpy as jnp
from jax import lax
from jax.experimental import pallas as pl
from jax.experimental.pallas import tpu as pltpu
from jax.sharding import PartitionSpec as P

BS = 128
CLASSES = 64

base_cost = 0.05
far_below = -1e30
LOW_ROWS = 16
KERNEL_BYTES = 32 * 1024 * 1024
MESH = pl.DeviceIdType.MESH


def loop(low, high, body, carry):
    if high - low <= 8:
        for index in range(low, high):
            carry = body(index, carry)
        return carry
    return lax.fori_loop(low, high, body, carry)


def kernel(
    sizes, src_hbm, dst_hbm, len_hbm, start_hbm, final_hbm, cong_hbm, cap_hbm, trans_hbm,
    dens_out, mean_out, val_out,
    src_s, dst_s, len_s,
    masses, values, cong, cap, trans, moving, weight, ceiling, edge_log, sums,
    dst_send, dst_recv, part_send, part_recv, back_send, back_recv, class_sums,
    in_sem, dst_ssem, dst_rsem, part_ssem, part_rsem, back_ssem, back_rsem,
    cong_ssem, cong_rsem, mean_ssem, mean_rsem,
):
    owners, sections, halves, per_peer, local_steps, block_count, class_count = sizes
    steps = sections * local_steps
    me = lax.axis_index("cells")
    section = lax.axis_index("tm")
    half = lax.axis_index("cls")
    groups = class_count // LOW_ROWS
    columns = [slice(b * BS, (b + 1) * BS) for b in range(block_count)]

    def after(axis, size, by):
        return {axis: lax.rem(lax.axis_index(axis) + by, size)}

    barrier = pltpu.get_barrier_semaphore()
    greeted = 0
    for axis, size in (("cells", owners), ("tm", sections), ("cls", halves)):

        def greet(by, carry, axis=axis, size=size):
            pl.semaphore_signal(
                barrier, inc=1, device_id=after(axis, size, by), device_id_type=MESH
            )
            return carry

        loop(1, size, greet, 0)
        greeted += size - 1

    own_cong = cong.at[section]
    scalar_loads = [
        pltpu.make_async_copy(src_hbm, src_s, in_sem.at[5]),
        pltpu.make_async_copy(dst_hbm, dst_s, in_sem.at[6]),
        pltpu.make_async_copy(len_hbm, len_s, in_sem.at[7]),
    ]
    loads = [
        pltpu.make_async_copy(cong_hbm, own_cong, in_sem.at[0]),
        pltpu.make_async_copy(cap_hbm, cap, in_sem.at[1]),
        pltpu.make_async_copy(final_hbm, values, in_sem.at[2]),
        pltpu.make_async_copy(start_hbm, masses, in_sem.at[3]),
        pltpu.make_async_copy(trans_hbm, trans, in_sem.at[4]),
    ]
    for load in scalar_loads + loads:
        load.start()
    for load in scalar_loads:
        load.wait()

    def target_rows(by, carry):
        peer = lax.rem(me + by, owners)
        for s in range(per_peer):
            target = jnp.where(s < len_s[peer], dst_s[peer * per_peer + s], -1)
            dst_send[by, s : s + 1, :] = jnp.full((1, BS), target, jnp.int32)
        return carry

    loop(0, owners, target_rows, 0)
    dst_recv[0] = dst_send[0]
    pl.semaphore_wait(barrier, greeted)

    def dst_copy(by):
        return pltpu.make_async_remote_copy(
            src_ref=dst_send.at[by], dst_ref=dst_recv.at[by],
            send_sem=dst_ssem.at[by], recv_sem=dst_rsem.at[by],
            device_id=after("cells", owners, by), device_id_type=MESH,
        )

    def cong_copy(by):
        return pltpu.make_async_remote_copy(
            src_ref=cong_hbm, dst_ref=cong.at[section],
            send_sem=cong_ssem.at[by], recv_sem=cong_rsem.at[section],
            device_id=after("tm", sections, by), device_id_type=MESH,
        )

    def cong_arrival(owner):
        return pltpu.make_async_remote_copy(
            src_ref=cong_hbm, dst_ref=cong.at[owner],
            send_sem=cong_ssem.at[0], recv_sem=cong_rsem.at[owner],
            device_id=after("tm", sections, 1), device_id_type=MESH,
        )

    def part_copy(r, by):
        return pltpu.make_async_remote_copy(
            src_ref=part_send.at[r, by], dst_ref=part_recv.at[r, by],
            send_sem=part_ssem.at[r, by], recv_sem=part_rsem.at[r, by],
            device_id=after("cells", owners, by), device_id_type=MESH,
        )

    def back_copy(r, by):
        return pltpu.make_async_remote_copy(
            src_ref=back_send.at[r, by], dst_ref=back_recv.at[r, by],
            send_sem=back_ssem.at[r, by], recv_sem=back_rsem.at[r, by],
            device_id=after("cells", owners, owners - by), device_id_type=MESH,
        )

    def mean_copy(by):
        return pltpu.make_async_remote_copy(
            src_ref=class_sums.at[0], dst_ref=class_sums.at[by],
            send_sem=mean_ssem.at[by], recv_sem=mean_rsem.at[by],
            device_id=after("cls", halves, by), device_id_type=MESH,
        )

    def started(copy):
        def body(by, carry):
            copy(by).start()
            return carry

        return body

    def sent(copy):
        def body(by, carry):
            copy(by).wait_send()
            return carry

        return body

    loop(1, sections, started(cong_copy), 0)
    loop(1, owners, started(dst_copy), 0)

    def one_loading(step, b):
        owner, local = divmod(step, local_steps)
        return cong[owner, local : local + 1, columns[b]] / cap[:, columns[b]]

    def forward_send(r):
        owner, local = divmod(r, local_steps)
        if owner < sections - 1 and local == 0:

            @pl.when(section > owner)
            def _():
                cong_arrival(owner).wait_recv()

        for b in range(block_count):
            mobility = 1.0 / (1.0 + one_loading(r, b))
            now = masses[:, columns[b]]
            moving[b] = (now * mobility).astype(jnp.bfloat16)
            masses[:, columns[b]] = now * (1.0 - mobility)

        def one_peer(by, carry):
            peer = lax.rem(me + by, owners)
            into = part_recv if isinstance(by, int) and by == 0 else part_send
            for s in range(per_peer):
                e = peer * per_peer + s
                into[r, by, s] = jnp.dot(
                    moving[src_s[e]], trans[e], preferred_element_type=jnp.float32
                ).astype(jnp.bfloat16)
            if into is part_send:
                part_copy(r, by).start()
            return carry

        loop(1, owners, one_peer, 0)
        one_peer(0, 0)

    def forward_receive(r):
        owner, local = divmod(r, local_steps)

        def one_source(by, totals):
            if not (isinstance(by, int) and by == 0):
                part_copy(r, by).wait_recv()
            totals = list(totals)
            for s in range(per_peer):
                row = jnp.broadcast_to(dst_recv[by, s : s + 1, :], (class_count, BS))
                part = part_recv[r, by, s].astype(jnp.float32)
                for b in range(block_count):
                    totals[b] = totals[b] + jnp.where(row == b, part, 0.0)
            return tuple(totals)

        totals = one_source(0, tuple(masses[:, c] for c in columns))
        totals = loop(1, owners, one_source, totals)
        for b in range(block_count):
            masses[:, columns[b]] = totals[b]

        @pl.when(section == owner)
        def _():
            for b in range(block_count):
                total = masses[:, columns[b]]
                dens_out[local, :, columns[b]] = total
                class_sums[0, local : local + 1, columns[b]] = jnp.sum(
                    total, axis=0, keepdims=True
                )
            if local == local_steps - 1:
                loop(1, halves, started(mean_copy), 0)

    def backward_send(r):
        lane = lax.broadcasted_iota(jnp.int32, (LOW_ROWS, BS), 1)
        lows = jnp.zeros((LOW_ROWS, BS), jnp.float32)
        for b in range(block_count):
            now = values[:, columns[b]]
            low = jnp.min(now, axis=1, keepdims=True)
            low = low.astype(jnp.bfloat16).astype(jnp.float32)
            weight[b] = jnp.exp(low - now)
            for g in range(groups):
                part = low[g * LOW_ROWS : (g + 1) * LOW_ROWS]
                lows = jnp.where(lane == g * block_count + b, part, lows)
        lows = lows.astype(jnp.bfloat16)

        def one_source(by, carry):
            here = isinstance(by, int) and by == 0
            into = back_recv if here else back_send
            if r == 0 and not here:
                dst_copy(by).wait_recv()
            for s in range(per_peer):
                row = jnp.broadcast_to(dst_recv[by, s : s + 1, :], (class_count, BS))
                picked = jnp.zeros((class_count, BS), jnp.float32)
                for b in range(block_count):
                    picked = jnp.where(row == b, weight[b], picked)
                into[r, by, s * class_count : (s + 1) * class_count] = picked.astype(jnp.bfloat16)
            into[r, by, per_peer * class_count :] = lows
            if not here:
                back_copy(r, by).start()
            return carry

        loop(1, owners, one_source, 0)
        one_source(0, 0)

    def backward_receive(r):
        step = steps - 1 - r
        owner, local = divmod(step, local_steps)
        lane = lax.broadcasted_iota(jnp.int32, (LOW_ROWS, BS), 1)

        def one_peer(by, tops):
            if not (isinstance(by, int) and by == 0):
                back_copy(r, by).wait_recv()
            peer = lax.rem(me + by, owners)
            tops = list(tops)
            lows = back_recv[r, by, per_peer * class_count :].astype(jnp.float32)
            for s in range(per_peer):
                e = peer * per_peer + s
                low = jnp.concatenate(
                    [
                        jnp.sum(
                            jnp.where(lane == g * block_count + dst_s[e], lows, 0.0),
                            axis=1,
                            keepdims=True,
                        )
                        for g in range(groups)
                    ],
                    axis=0,
                )
                log = jnp.where(s < len_s[peer], -low, far_below)
                log = jnp.broadcast_to(log, (class_count, BS))
                edge_log[by * per_peer + s] = log
                sums[by * per_peer + s] = lax.dot_general(
                    back_recv[r, by, s * class_count : (s + 1) * class_count], trans[e], (((1,), (1,)), ((), ())),
                    preferred_element_type=jnp.float32,
                )
                for b in range(block_count):
                    tops[b] = jnp.maximum(tops[b], jnp.where(src_s[e] == b, log, far_below))
            return tuple(tops)

        tops = one_peer(0, tuple(-values[:, c] for c in columns))
        tops = loop(1, owners, one_peer, tops)
        for b in range(block_count):
            ceiling[b] = tops[b]

        def one_total(by, totals):
            peer = lax.rem(me + by, owners)
            totals = list(totals)
            for s in range(per_peer):
                source = src_s[peer * per_peer + s]
                place = by * per_peer + s
                term = jnp.exp(edge_log[place] - ceiling[source]) * sums[place]
                for b in range(block_count):
                    totals[b] = totals[b] + jnp.where(source == b, term, 0.0)
            return tuple(totals)

        if owner > 0 and local == local_steps - 1:

            @pl.when(section < owner)
            def _():
                cong_arrival(owner).wait_recv()

        totals = tuple(jnp.exp(-values[:, columns[b]] - ceiling[b]) for b in range(block_count))
        totals = loop(0, owners, one_total, totals)
        for b in range(block_count):
            travel = base_cost * (1.0 + one_loading(step, b))
            values[:, columns[b]] = travel - (ceiling[b] + jnp.log(totals[b]))

        @pl.when(section == owner)
        def _():
            for b in range(block_count):
                val_out[local, :, columns[b]] = values[:, columns[b]]

    for load in loads:
        load.wait()

    def forward_guard(r, body):
        owner = r // local_steps
        if owner == 0:
            body(r)
        else:

            @pl.when(section >= owner)
            def _():
                body(r)


    def backward_guard(r, body):
        owner = (steps - 1 - r) // local_steps
        if owner == sections - 1:
            body(r)
        else:

            @pl.when(section <= owner)
            def _():
                body(r)


    forward_guard(0, forward_send)
    backward_guard(0, backward_send)
    for r in range(steps):
        forward_guard(r, forward_receive)
        if r + 1 < steps:
            forward_guard(r + 1, forward_send)
        backward_guard(r, backward_receive)
        if r + 1 < steps:
            backward_guard(r + 1, backward_send)

    def arrived(by, carry):
        mean_copy(by).wait_recv()
        return carry

    loop(1, halves, arrived, 0)
    total = class_sums[half]
    for index in range(1, halves):
        total = total + class_sums[lax.rem(half - index + halves, halves)]
    mean_out[...] = total / CLASSES

    loop(1, sections, sent(cong_copy), 0)
    loop(1, owners, sent(dst_copy), 0)
    loop(1, halves, sent(mean_copy), 0)
    for r in range(steps):
        forward_guard(r, lambda r: loop(1, owners, sent(functools.partial(part_copy, r)), 0))
        backward_guard(r, lambda r: loop(1, owners, sent(functools.partial(back_copy, r)), 0))


def write_out(dens_in, mean_in, val_in, dens_out, mean_out, val_out, sem):
    copies = [
        pltpu.make_async_copy(dens_in, dens_out, sem.at[0]),
        pltpu.make_async_copy(val_in, val_out, sem.at[1]),
        pltpu.make_async_copy(mean_in, mean_out, sem.at[2]),
    ]
    for copy in copies:
        copy.start()
    for copy in copies:
        copy.wait()


def shards(
    start_density, final_value, congestion, capacity, trans_values, src_local, dst_local, bucket_len
):
    owners = lax.axis_size("cells")
    sections = lax.axis_size("tm")
    halves = lax.axis_size("cls")
    class_count, cell_count = start_density.shape
    local_steps = congestion.shape[0]
    block_count = cell_count // BS
    edge_count = src_local.shape[0]
    per_peer = edge_count // owners
    steps = sections * local_steps
    sizes = (owners, sections, halves, per_peer, local_steps, block_count, class_count)
    held = pl.BlockSpec(memory_space=pltpu.VMEM)
    far = pl.BlockSpec(memory_space=pltpu.HBM)
    whole = pl.BlockSpec(memory_space=pl.ANY)
    f32, bf16 = jnp.float32, jnp.bfloat16
    tile = (class_count, BS)
    results = (
        jax.ShapeDtypeStruct((local_steps, class_count, cell_count), f32),
        jax.ShapeDtypeStruct((local_steps, cell_count), f32),
        jax.ShapeDtypeStruct((local_steps, class_count, cell_count), f32),
    )
    computed = pl.pallas_call(
        functools.partial(kernel, sizes),
        out_shape=tuple(pltpu.VMEM(r.shape, r.dtype) for r in results),
        in_specs=[far] * 8,
        out_specs=(held, held, held),
        scratch_shapes=[
            pltpu.SMEM((edge_count,), jnp.int32),
            pltpu.SMEM((edge_count,), jnp.int32),
            pltpu.SMEM((owners,), jnp.int32),
            pltpu.VMEM((class_count, cell_count), f32),
            pltpu.VMEM((class_count, cell_count), f32),
            pltpu.VMEM((sections, local_steps, cell_count), f32),
            pltpu.VMEM((1, cell_count), f32),
            pltpu.VMEM((edge_count, BS, BS), bf16),
            pltpu.VMEM((block_count, *tile), bf16),
            pltpu.VMEM((block_count, *tile), f32),
            pltpu.VMEM((block_count, *tile), f32),
            pltpu.VMEM((edge_count, *tile), f32),
            pltpu.VMEM((edge_count, *tile), f32),
            pltpu.VMEM((owners, per_peer, BS), jnp.int32),
            pltpu.VMEM((owners, per_peer, BS), jnp.int32),
            pltpu.VMEM((steps, owners, per_peer, *tile), bf16),
            pltpu.VMEM((steps, owners, per_peer, *tile), bf16),
            pltpu.VMEM((steps, owners, per_peer * class_count + LOW_ROWS, BS), bf16),
            pltpu.VMEM((steps, owners, per_peer * class_count + LOW_ROWS, BS), bf16),
            pltpu.VMEM((halves, local_steps, cell_count), f32),
            pltpu.SemaphoreType.DMA((8,)),
            pltpu.SemaphoreType.DMA((owners,)),
            pltpu.SemaphoreType.DMA((owners,)),
            pltpu.SemaphoreType.DMA((steps, owners)),
            pltpu.SemaphoreType.DMA((steps, owners)),
            pltpu.SemaphoreType.DMA((steps, owners)),
            pltpu.SemaphoreType.DMA((steps, owners)),
            pltpu.SemaphoreType.DMA((sections,)),
            pltpu.SemaphoreType.DMA((sections,)),
            pltpu.SemaphoreType.DMA((halves,)),
            pltpu.SemaphoreType.DMA((halves,)),
        ],
        compiler_params=pltpu.CompilerParams(
            collective_id=0, has_side_effects=True, vmem_limit_bytes=KERNEL_BYTES
        ),
    )(*(
        pltpu.with_memory_space_constraint(operand, pltpu.HBM)
        for operand in (
            src_local, dst_local, bucket_len, start_density, final_value, congestion,
            capacity.reshape(1, cell_count), trans_values,
        )
    ))
    return pl.pallas_call(
        write_out,
        out_shape=results,
        in_specs=[whole] * 3,
        out_specs=[whole] * 3,
        scratch_shapes=[pltpu.SemaphoreType.DMA((3,))],
        compiler_params=pltpu.CompilerParams(vmem_limit_bytes=1024 * 1024),
    )(*(pltpu.with_memory_space_constraint(part, pltpu.VMEM) for part in computed))


def solution(mesh):
    in_specs = (
        P(("groups", "cls"), "cells"),
        P(("groups", "cls"), "cells"),
        P(("groups", "tm"), "cells"),
        P(("groups", "cells")),
        P(("groups", "cells"), None, None),
        P(("groups", "cells")),
        P(("groups", "cells")),
        P(("groups", "cells")),
    )
    out_specs = (
        P(("groups", "tm"), "cls", "cells"),
        P(("groups", "tm"), "cells"),
        P(("groups", "tm"), "cls", "cells"),
    )
    return jax.shard_map(shards, mesh=mesh, in_specs=in_specs, out_specs=out_specs, check_vma=False)
```

```python
import functools

import jax
import jax.numpy as jnp
from jax import lax
from jax.experimental import pallas as pl
from jax.experimental.pallas import tpu as pltpu
from jax.sharding import PartitionSpec as P

BS = 128
CLASSES = 64

base_cost = 0.05
far_below = -1e30
LOW_ROWS = 16
KERNEL_BYTES = 32 * 1024 * 1024
MESH = pl.DeviceIdType.MESH


def loop(low, high, body, carry):
    if high - low <= 8:
        for index in range(low, high):
            carry = body(index, carry)
        return carry
    return lax.fori_loop(low, high, body, carry)


def kernel(
    sizes, src_hbm, dst_hbm, len_hbm, start_hbm, final_hbm, cong_hbm, cap_hbm, trans_hbm,
    dens_out, mean_out, val_out,
    src_s, dst_s, len_s,
    start, final, density, value, stay, cong, cap, trans, moving, weight, ceiling, edge_log, sums,
    dst_send, dst_recv, part_send, part_recv, back_send, back_recv, sums_send, class_sums,
    in_sem, dst_ssem, dst_rsem, part_ssem, part_rsem, back_ssem, back_rsem,
    cong_ssem, cong_rsem, mean_ssem, mean_rsem,
    dens_ssem, dens_rsem, val_ssem, val_rsem,
):
    owners, sections, halves, per_peer, local_steps, block_count, class_count = sizes
    steps = sections * local_steps
    me = lax.axis_index("cells")
    section = lax.axis_index("tm")
    half = lax.axis_index("cls")
    groups = class_count // LOW_ROWS
    columns = [slice(b * BS, (b + 1) * BS) for b in range(block_count)]

    def after(axis, size, by):
        return {axis: lax.rem(lax.axis_index(axis) + by, size)}

    barrier = pltpu.get_barrier_semaphore()
    def greet(by, carry):
        pl.semaphore_signal(
            barrier, inc=1, device_id=after("cells", owners, by), device_id_type=MESH
        )
        return carry

    def greet_beside(by, carry):
        pl.semaphore_signal(
            barrier,
            inc=1,
            device_id={
                "tm": lax.rem(section + by // halves, sections),
                "cls": lax.rem(half + by % halves, halves),
            },
            device_id_type=MESH,
        )
        return carry

    loop(1, owners, greet, 0)
    loop(1, sections * halves, greet_beside, 0)
    greeted = owners - 1 + sections * halves - 1

    own_cong = cong.at[section]
    scalar_loads = [
        pltpu.make_async_copy(src_hbm, src_s, in_sem.at[5]),
        pltpu.make_async_copy(dst_hbm, dst_s, in_sem.at[6]),
        pltpu.make_async_copy(len_hbm, len_s, in_sem.at[7]),
    ]
    loads = [
        pltpu.make_async_copy(cong_hbm, own_cong, in_sem.at[0]),
        pltpu.make_async_copy(cap_hbm, cap, in_sem.at[1]),
        pltpu.make_async_copy(final_hbm, final, in_sem.at[2]),
        pltpu.make_async_copy(start_hbm, start, in_sem.at[3]),
        pltpu.make_async_copy(trans_hbm, trans, in_sem.at[4]),
    ]
    for load in scalar_loads + loads:
        load.start()
    for load in scalar_loads:
        load.wait()

    def target_rows(by, carry):
        peer = lax.rem(me + by, owners)
        for s in range(per_peer):
            target = jnp.where(s < len_s[peer], dst_s[peer * per_peer + s], -1)
            dst_send[by, s : s + 1, :] = jnp.full((1, BS), target, jnp.int32)
        return carry

    loop(0, owners, target_rows, 0)
    dst_recv[0] = dst_send[0]
    pl.semaphore_wait(barrier, greeted)

    def dst_copy(by):
        return pltpu.make_async_remote_copy(
            src_ref=dst_send.at[by], dst_ref=dst_recv.at[by],
            send_sem=dst_ssem.at[by], recv_sem=dst_rsem.at[by],
            device_id=after("cells", owners, by), device_id_type=MESH,
        )

    def cong_copy(target):
        return pltpu.make_async_remote_copy(
            src_ref=cong_hbm, dst_ref=cong.at[section],
            send_sem=cong_ssem.at[target], recv_sem=cong_rsem.at[section],
            device_id={"tm": target}, device_id_type=MESH,
        )

    def cong_arrival(owner):
        return pltpu.make_async_remote_copy(
            src_ref=cong_hbm, dst_ref=cong.at[owner],
            send_sem=cong_ssem.at[0], recv_sem=cong_rsem.at[owner],
            device_id={"tm": lax.rem(section + 1, sections)}, device_id_type=MESH,
        )

    def dens_copy(step):
        owner, local = divmod(step, local_steps)
        return pltpu.make_async_remote_copy(
            src_ref=density.at[step], dst_ref=dens_out.at[local],
            send_sem=dens_ssem.at[step], recv_sem=dens_rsem.at[local],
            device_id={"tm": owner}, device_id_type=MESH,
        )

    def val_copy(step):
        owner, local = divmod(step, local_steps)
        return pltpu.make_async_remote_copy(
            src_ref=value.at[step], dst_ref=val_out.at[local],
            send_sem=val_ssem.at[step], recv_sem=val_rsem.at[local],
            device_id={"tm": owner}, device_id_type=MESH,
        )

    def mean_copy(step, by):
        owner, local = divmod(step, local_steps)
        return pltpu.make_async_remote_copy(
            src_ref=sums_send.at[step], dst_ref=class_sums.at[half, local],
            send_sem=mean_ssem.at[step, by], recv_sem=mean_rsem.at[half, local],
            device_id={"tm": owner, "cls": lax.rem(half + by, halves)}, device_id_type=MESH,
        )

    def part_copy(r, by):
        return pltpu.make_async_remote_copy(
            src_ref=part_send.at[r, by], dst_ref=part_recv.at[r, by],
            send_sem=part_ssem.at[r, by], recv_sem=part_rsem.at[r, by],
            device_id=after("cells", owners, by), device_id_type=MESH,
        )

    def back_copy(r, by):
        return pltpu.make_async_remote_copy(
            src_ref=back_send.at[r, by], dst_ref=back_recv.at[r, by],
            send_sem=back_ssem.at[r, by], recv_sem=back_rsem.at[r, by],
            device_id=after("cells", owners, owners - by), device_id_type=MESH,
        )

    def started(copy):
        def body(by, carry):
            copy(by).start()
            return carry

        return body

    def sent(copy):
        def body(by, carry):
            copy(by).wait_send()
            return carry

        return body

    loop(1, owners, started(dst_copy), 0)
    ends = sorted({0, sections - 1}) if sections > 1 else []
    for target in ends:

        @pl.when(section != target)
        def _(target=target):
            cong_copy(target).start()


    def one_loading(step, b):
        owner, local = divmod(step, local_steps)
        return cong[owner, local : local + 1, columns[b]] / cap[:, columns[b]]

    def forward_send(r):
        owner, local = divmod(r, local_steps)
        if owner < sections - 1 and local == 0:
            cong_arrival(owner).wait_recv()
        masses = start if r == 0 else density.at[r - 1]
        for b in range(block_count):
            mobility = 1.0 / (1.0 + one_loading(r, b))
            now = masses[:, columns[b]]
            moving[b] = (now * mobility).astype(jnp.bfloat16)
            stay[:, columns[b]] = now * (1.0 - mobility)

        def one_peer(by, carry):
            peer = lax.rem(me + by, owners)
            into = part_recv if isinstance(by, int) and by == 0 else part_send
            for s in range(per_peer):
                e = peer * per_peer + s
                into[r, by, s] = jnp.dot(
                    moving[src_s[e]], trans[e], preferred_element_type=jnp.float32
                ).astype(jnp.bfloat16)
            if into is part_send:
                part_copy(r, by).start()
            return carry

        loop(1, owners, one_peer, 0)
        one_peer(0, 0)

    def forward_receive(r):
        owner, local = divmod(r, local_steps)

        def one_source(by, totals):
            if not (isinstance(by, int) and by == 0):
                if r == 0 and sections > 1:
                    dst_copy(by).wait_recv()
                part_copy(r, by).wait_recv()
            totals = list(totals)
            for s in range(per_peer):
                row = jnp.broadcast_to(dst_recv[by, s : s + 1, :], (class_count, BS))
                part = part_recv[r, by, s].astype(jnp.float32)
                for b in range(block_count):
                    totals[b] = totals[b] + jnp.where(row == b, part, 0.0)
            return tuple(totals)

        totals = one_source(0, tuple(stay[:, c] for c in columns))
        totals = loop(1, owners, one_source, totals)
        for b in range(block_count):
            if owner == sections - 1:
                dens_out[local, :, columns[b]] = totals[b]
            if r + 1 < steps:
                density[r, :, columns[b]] = totals[b]
        if owner < sections - 1:
            dens_copy(r).start()
        for b in range(block_count):
            sums_send[r, :, columns[b]] = jnp.sum(totals[b], axis=0, keepdims=True)
        if owner == sections - 1:
            class_sums[half, local] = sums_send[r]
        loop(int(owner == sections - 1), halves, started(functools.partial(mean_copy, r)), 0)

    def backward_send(r):
        values = final if r == 0 else value.at[steps - r]
        lane = lax.broadcasted_iota(jnp.int32, (LOW_ROWS, BS), 1)
        lows = jnp.zeros((LOW_ROWS, BS), jnp.float32)
        for b in range(block_count):
            now = values[:, columns[b]]
            low = jnp.min(now, axis=1, keepdims=True)
            low = low.astype(jnp.bfloat16).astype(jnp.float32)
            weight[b] = jnp.exp(low - now)
            for g in range(groups):
                part = low[g * LOW_ROWS : (g + 1) * LOW_ROWS]
                lows = jnp.where(lane == g * block_count + b, part, lows)
        lows = lows.astype(jnp.bfloat16)

        def one_source(by, carry):
            here = isinstance(by, int) and by == 0
            into = back_recv if here else back_send
            if r == 0 and not here:
                dst_copy(by).wait_recv()
            for s in range(per_peer):
                row = jnp.broadcast_to(dst_recv[by, s : s + 1, :], (class_count, BS))
                picked = jnp.zeros((class_count, BS), jnp.float32)
                for b in range(block_count):
                    picked = jnp.where(row == b, weight[b], picked)
                into[r, by, s * class_count : (s + 1) * class_count] = picked.astype(jnp.bfloat16)
            into[r, by, per_peer * class_count :] = lows
            if not here:
                back_copy(r, by).start()
            return carry

        loop(1, owners, one_source, 0)
        one_source(0, 0)

    def backward_receive(r):
        step = steps - 1 - r
        owner, local = divmod(step, local_steps)
        values = final if r == 0 else value.at[step + 1]
        lane = lax.broadcasted_iota(jnp.int32, (LOW_ROWS, BS), 1)

        def one_peer(by, tops):
            if not (isinstance(by, int) and by == 0):
                back_copy(r, by).wait_recv()
            peer = lax.rem(me + by, owners)
            tops = list(tops)
            lows = back_recv[r, by, per_peer * class_count :].astype(jnp.float32)
            for s in range(per_peer):
                e = peer * per_peer + s
                low = jnp.concatenate(
                    [
                        jnp.sum(
                            jnp.where(lane == g * block_count + dst_s[e], lows, 0.0),
                            axis=1,
                            keepdims=True,
                        )
                        for g in range(groups)
                    ],
                    axis=0,
                )
                log = jnp.where(s < len_s[peer], -low, far_below)
                log = jnp.broadcast_to(log, (class_count, BS))
                edge_log[by * per_peer + s] = log
                sums[by * per_peer + s] = lax.dot_general(
                    back_recv[r, by, s * class_count : (s + 1) * class_count], trans[e], (((1,), (1,)), ((), ())),
                    preferred_element_type=jnp.float32,
                )
                for b in range(block_count):
                    tops[b] = jnp.maximum(tops[b], jnp.where(src_s[e] == b, log, far_below))
            return tuple(tops)

        tops = one_peer(0, tuple(-values[:, c] for c in columns))
        tops = loop(1, owners, one_peer, tops)
        for b in range(block_count):
            ceiling[b] = tops[b]

        def one_total(by, totals):
            peer = lax.rem(me + by, owners)
            totals = list(totals)
            for s in range(per_peer):
                source = src_s[peer * per_peer + s]
                place = by * per_peer + s
                term = jnp.exp(edge_log[place] - ceiling[source]) * sums[place]
                for b in range(block_count):
                    totals[b] = totals[b] + jnp.where(source == b, term, 0.0)
            return tuple(totals)

        if owner > 0 and local == local_steps - 1:
            cong_arrival(owner).wait_recv()

        totals = tuple(jnp.exp(-values[:, columns[b]] - ceiling[b]) for b in range(block_count))
        totals = loop(0, owners, one_total, totals)
        for b in range(block_count):
            travel = base_cost * (1.0 + one_loading(step, b))
            result = travel - (ceiling[b] + jnp.log(totals[b]))
            if owner == 0:
                val_out[local, :, columns[b]] = result
            if step > 0:
                value[step, :, columns[b]] = result
        if owner > 0:
            val_copy(step).start()

    for load in loads:
        load.wait()

    @pl.when(section == sections - 1)
    def _():
        for r in range(steps):
            forward_send(r)
            forward_receive(r)

    @pl.when(section == 0)
    def _():
        for r in range(steps):
            backward_send(r)
            backward_receive(r)

    def dst_arrived(by, carry):
        dst_copy(by).wait_recv()
        return carry

    if sections > 2:

        @pl.when((section > 0) & (section < sections - 1))
        def _():
            loop(1, owners, dst_arrived, 0)

    for local in range(local_steps):

        def arrived(source, carry, local=local):
            pltpu.make_async_remote_copy(
                src_ref=sums_send.at[local], dst_ref=class_sums.at[source, local],
                send_sem=mean_ssem.at[0, 0], recv_sem=mean_rsem.at[source, local],
                device_id=after("cls", halves, 1), device_id_type=MESH,
            ).wait_recv()
            return carry

        def arrived_beside(by, carry, arrived=arrived):
            return arrived(lax.rem(half + by, halves), carry)

        loop(1, halves, arrived_beside, 0)
        if sections > 1:

            @pl.when(section != sections - 1)
            def _(arrived=arrived, local=local):
                arrived(half, 0)
                dens_copy(local).wait_recv()

            @pl.when(section != 0)
            def _(local=local):
                val_copy(steps - local_steps + local).wait_recv()

        total = class_sums[0, local]
        for index in range(1, halves):
            total = total + class_sums[index, local]
        mean_out[local : local + 1, :] = total / CLASSES

    loop(1, owners, sent(dst_copy), 0)
    for target in ends:

        @pl.when(section != target)
        def _(target=target):
            cong_copy(target).wait_send()

    @pl.when(section == sections - 1)
    def _():
        for r in range(steps):
            owner = r // local_steps
            loop(1, owners, sent(functools.partial(part_copy, r)), 0)
            loop(int(owner == sections - 1), halves, sent(functools.partial(mean_copy, r)), 0)
            if owner < sections - 1:
                dens_copy(r).wait_send()

    @pl.when(section == 0)
    def _():
        for r in range(steps):
            step = steps - 1 - r
            loop(1, owners, sent(functools.partial(back_copy, r)), 0)
            if step // local_steps > 0:
                val_copy(step).wait_send()


def write_out(dens_in, mean_in, val_in, dens_out, mean_out, val_out, sem):
    copies = [
        pltpu.make_async_copy(dens_in, dens_out, sem.at[0]),
        pltpu.make_async_copy(val_in, val_out, sem.at[1]),
        pltpu.make_async_copy(mean_in, mean_out, sem.at[2]),
    ]
    for copy in copies:
        copy.start()
    for copy in copies:
        copy.wait()


def shards(
    start_density, final_value, congestion, capacity, trans_values, src_local, dst_local, bucket_len
):
    owners = lax.axis_size("cells")
    sections = lax.axis_size("tm")
    halves = lax.axis_size("cls")
    class_count, cell_count = start_density.shape
    local_steps = congestion.shape[0]
    block_count = cell_count // BS
    edge_count = src_local.shape[0]
    per_peer = edge_count // owners
    steps = sections * local_steps
    sizes = (owners, sections, halves, per_peer, local_steps, block_count, class_count)
    held = pl.BlockSpec(memory_space=pltpu.VMEM)
    far = pl.BlockSpec(memory_space=pltpu.HBM)
    whole = pl.BlockSpec(memory_space=pl.ANY)
    f32, bf16 = jnp.float32, jnp.bfloat16
    tile = (class_count, BS)
    results = (
        jax.ShapeDtypeStruct((local_steps, class_count, cell_count), f32),
        jax.ShapeDtypeStruct((local_steps, cell_count), f32),
        jax.ShapeDtypeStruct((local_steps, class_count, cell_count), f32),
    )
    computed = pl.pallas_call(
        functools.partial(kernel, sizes),
        out_shape=tuple(pltpu.VMEM(r.shape, r.dtype) for r in results),
        in_specs=[far] * 8,
        out_specs=(held, held, held),
        scratch_shapes=[
            pltpu.SMEM((edge_count,), jnp.int32),
            pltpu.SMEM((edge_count,), jnp.int32),
            pltpu.SMEM((owners,), jnp.int32),
            pltpu.VMEM((class_count, cell_count), f32),
            pltpu.VMEM((class_count, cell_count), f32),
            pltpu.VMEM((steps, class_count, cell_count), f32),
            pltpu.VMEM((steps, class_count, cell_count), f32),
            pltpu.VMEM((class_count, cell_count), f32),
            pltpu.VMEM((sections, local_steps, cell_count), f32),
            pltpu.VMEM((1, cell_count), f32),
            pltpu.VMEM((edge_count, BS, BS), bf16),
            pltpu.VMEM((block_count, *tile), bf16),
            pltpu.VMEM((block_count, *tile), f32),
            pltpu.VMEM((block_count, *tile), f32),
            pltpu.VMEM((edge_count, *tile), f32),
            pltpu.VMEM((edge_count, *tile), f32),
            pltpu.VMEM((owners, per_peer, BS), jnp.int32),
            pltpu.VMEM((owners, per_peer, BS), jnp.int32),
            pltpu.VMEM((steps, owners, per_peer, *tile), bf16),
            pltpu.VMEM((steps, owners, per_peer, *tile), bf16),
            pltpu.VMEM((steps, owners, per_peer * class_count + LOW_ROWS, BS), bf16),
            pltpu.VMEM((steps, owners, per_peer * class_count + LOW_ROWS, BS), bf16),
            pltpu.VMEM((steps, 1, cell_count), f32),
            pltpu.VMEM((halves, local_steps, 1, cell_count), f32),
            pltpu.SemaphoreType.DMA((8,)),
            pltpu.SemaphoreType.DMA((owners,)),
            pltpu.SemaphoreType.DMA((owners,)),
            pltpu.SemaphoreType.DMA((steps, owners)),
            pltpu.SemaphoreType.DMA((steps, owners)),
            pltpu.SemaphoreType.DMA((steps, owners)),
            pltpu.SemaphoreType.DMA((steps, owners)),
            pltpu.SemaphoreType.DMA((sections,)),
            pltpu.SemaphoreType.DMA((sections,)),
            pltpu.SemaphoreType.DMA((steps, halves)),
            pltpu.SemaphoreType.DMA((halves, local_steps)),
            pltpu.SemaphoreType.DMA((steps,)),
            pltpu.SemaphoreType.DMA((local_steps,)),
            pltpu.SemaphoreType.DMA((steps,)),
            pltpu.SemaphoreType.DMA((local_steps,)),
        ],
        compiler_params=pltpu.CompilerParams(
            collective_id=0, has_side_effects=True, vmem_limit_bytes=KERNEL_BYTES
        ),
    )(*(
        pltpu.with_memory_space_constraint(operand, pltpu.HBM)
        for operand in (
            src_local, dst_local, bucket_len, start_density, final_value, congestion,
            capacity.reshape(1, cell_count), trans_values,
        )
    ))
    return pl.pallas_call(
        write_out,
        out_shape=results,
        in_specs=[whole] * 3,
        out_specs=[whole] * 3,
        scratch_shapes=[pltpu.SemaphoreType.DMA((3,))],
        compiler_params=pltpu.CompilerParams(vmem_limit_bytes=1024 * 1024),
    )(*(pltpu.with_memory_space_constraint(part, pltpu.VMEM) for part in computed))


def solution(mesh):
    in_specs = (
        P(("groups", "cls"), "cells"),
        P(("groups", "cls"), "cells"),
        P(("groups", "tm"), "cells"),
        P(("groups", "cells")),
        P(("groups", "cells"), None, None),
        P(("groups", "cells")),
        P(("groups", "cells")),
        P(("groups", "cells")),
    )
    out_specs = (
        P(("groups", "tm"), "cls", "cells"),
        P(("groups", "tm"), "cells"),
        P(("groups", "tm"), "cls", "cells"),
    )
    return jax.shard_map(shards, mesh=mesh, in_specs=in_specs, out_specs=out_specs, check_vma=False)
```
